32 devices in a mesh: groups: 2 (over y), pack: 4 (over z), mp: 2 (over x), sub: 2 (over core).
Axes of the slice: x: 2, y: 2, z: 4, core: 2. Of those that a mesh axis runs over, the one named last changes fastest.
Arguments:
- frame_enc: bfloat16 [8192, 512], P(('groups', 'pack')), parts along dimension 0, may hold values from -400 to 400
- phrase_enc: bfloat16 [16384, 1024], P(('groups', 'pack', 'mp')), parts along dimension 0, may hold values from -6 to 6
- key_weight: bfloat16 [1024, 512], replicated, may hold values from -0.1875 to 0.1875
- out_weight: bfloat16 [512, 4096], P(None, ('mp', 'sub')), may hold values from -1.5 to 1.5
- gate_weight: float32 [512], replicated, may hold values from -0.5 to 0.5
- phrase_token: int32 [16384], P('groups'), parts along dimension 0, may hold values from 1 to 4095
- bias_blocks: int32 [8, 128], P('groups'), parts along dimension 0, may hold values from 0 to 127, as said below
- utt_lengths: int32 [8, 4], P(('groups', 'pack')), parts along dimension 0, may hold values from 1 to 512, 1024 in all within a row
- targets: int32 [8192], P(('groups', 'pack')), parts along dimension 0, may hold values from 0 to 4095
Outputs:
- loss: float32 [8192], P(('groups', 'pack')), parts along dimension 0
The draws below stay inside these ranges and needn't reach their ends.
There are 2 independent parts, one for each index of `groups`. The reference program is written for one: setup_inputs(seed, part) draws one part's arguments, and reference() takes and returns one part's arrays. A program takes and returns all parts, laid end to end along the dimension named above; an argument that names none is the same for every part. Nothing has to cross between parts.
Inputs may be any that keep to these rules, and one draw needn't show every extreme that they name: `bias_blocks`: in every row, at most 32 entries lie in one phrase shard (equal values of block // 16), and some shard gives exactly 32 entries to every row. `utt_lengths`: each row sums to 1024.
All inputs are finite; a program needn't handle non-finite values.
Results may differ from the reference program's by a relative error of at most 0.0016.
Values may be sent and summed in bfloat16 or wider, within the bound.
A program may use at most 128 MiB of HBM per device.

```python
import math
import jax
import jax.numpy as jnp
import numpy as np
from jax import lax

J = 512
E = 1024
V = 4096
BLK = 64
FR_DEV = 1024
PB_DEV = 16
UTT_DEV = 4
LIST = 32
FRAMES = 4096
PACKS = 4
SOURCES = 8
BLOCKS = 128
PHRASES = 8192
ENTRIES = 128
CAP = 32


def draw_frame_enc(key, part):
    key = jax.random.fold_in(key, 11)
    base_draw = jax.random.normal(key, (FRAMES, J), jnp.float32)
    return jnp.clip(base_draw, -6.0, 6.0).astype(jnp.bfloat16)


def draw_bias_blocks(key, part):
    key = jax.random.fold_in(key, 23)

    def one_row(row_key):
        hot_source = jax.random.randint(jax.random.fold_in(row_key, 1), (), 0, SOURCES)
        shuffled = jax.random.permutation(jax.random.fold_in(row_key, 2), CAP * SOURCES - CAP)
        picked = shuffled[:ENTRIES - CAP]
        slot_pick = picked + jnp.where(picked >= hot_source * CAP, CAP, 0)
        sources = jnp.concatenate([jnp.full((CAP,), hot_source, jnp.int32), (slot_pick // CAP).astype(jnp.int32)])
        sources = jax.random.permutation(jax.random.fold_in(row_key, 3), sources)
        inner_block = jax.random.randint(jax.random.fold_in(row_key, 4), (ENTRIES,), 0, PB_DEV)
        return sources * PB_DEV + inner_block
    row_keys = jax.random.split(key, PACKS)
    return jax.vmap(one_row)(row_keys).astype(jnp.int32)


def place_ends(drawn, own_key, least, largest):
    place = [jax.random.randint(jax.random.fold_in(own_key, axis), (), 0, length) for axis, length in enumerate(drawn.shape)]
    widest = drawn.shape.index(max(drawn.shape))
    beside = place[:widest] + [(place[widest] + 1) % drawn.shape[widest]] + place[widest + 1:]
    return drawn.at[tuple(place)].set(least).at[tuple(beside)].set(largest)


def levels(key, shape, cuts, least, top_value):
    gain = 1.0
    for dim, blocks in cuts:
        steps = jax.random.uniform(jax.random.fold_in(jax.random.fold_in(key, 6), dim), (blocks,), jnp.float32, least / len(cuts), top_value / len(cuts))
        gain = gain * jnp.repeat(jnp.exp(steps), shape[dim] // blocks).reshape((-1,) + (1,) * (len(shape) - 1 - dim))
    return gain


def length_profile(amount, total, most, lean):
    loads = [(1 << 20) // math.isqrt(standing ** lean) + 1 for standing in range(2, amount + 1)]
    spare, given = total - most - (amount - 1), [1] * (amount - 1)
    while spare > 0:
        free = [i for i in range(amount - 1) if given[i] < most]
        pool, budget = sum([loads[i] for i in free]), spare
        for i in free:
            addition = min(most - given[i], max(1, budget * loads[i] // pool), spare)
            given[i] = given[i] + addition
            spare = spare - addition
    return np.array([most] + given)


def ragged(own_key, count, total, most, skew):
    if count == 2:
        one = jax.random.randint(own_key, (), max(1, total - most), min(most, total - 1) + 1)
        return jnp.stack([one, total - one])
    tallies = jnp.asarray(length_profile(count, total, most, skew), jnp.int32)
    twos = (count - 1) // 2
    giver, taker = tallies[1:1 + 2 * twos:2], tallies[2:2 + 2 * twos:2]
    slack = jnp.minimum(giver - 1, most - taker)
    shifted = jax.random.randint(jax.random.fold_in(own_key, 1), (twos,), 0, 1 << 20) % (slack + 1)
    tallies = tallies.at[1:1 + 2 * twos:2].set(giver - shifted).at[2:2 + 2 * twos:2].set(taker + shifted)
    return tallies[jax.random.permutation(jax.random.fold_in(own_key, 2), count)]


def centred(rng, shape, spread, most, shards=(), kind=jnp.bfloat16):
    level = levels(rng, shape, shards, -0.22, 0.18) if shards else 1.0
    values = jax.random.normal(rng, shape, jnp.float32) * spread * level
    return jnp.minimum(jnp.maximum(values, -most), most).astype(kind)


def setup_inputs(seed: int = 0, part: int = 0) -> dict:
    arg_keys = jax.random.split(jax.random.key(seed), 10)
    part_keys = jax.random.split(jax.random.fold_in(arg_keys[9], part), 10)
    frame_enc = draw_frame_enc(jax.random.fold_in(jax.random.fold_in(arg_keys[9], part), 71), part)
    phrase_enc = centred(part_keys[1], (PHRASES, E), 1.0, 6.0, ((0, 8),))
    key_weight = centred(arg_keys[2], (E, J), E ** -0.5, 0.1875)
    out_weight = centred(arg_keys[3], (J, V), (J // 32) ** -0.5, 1.5, ((1, 4),))
    gate_weight = centred(arg_keys[4], (J,), (J // 4) ** -0.5, 0.5, (), jnp.float32)
    phrase_token = place_ends(jax.random.randint(part_keys[5], (PHRASES,), 1, V), jax.random.fold_in(part_keys[5], 1), 1, V - 1).astype(jnp.int32)
    bias_blocks = draw_bias_blocks(jax.random.fold_in(jax.random.fold_in(arg_keys[9], part), 71), part)
    utt_lengths = jax.vmap(lambda own: ragged(own, UTT_DEV, FR_DEV, FR_DEV // 2, 2))(jax.random.split(part_keys[7], PACKS)).reshape((PACKS, UTT_DEV)).astype(jnp.int32)
    targets = place_ends(jax.random.randint(part_keys[8], (FRAMES,), 0, V), jax.random.fold_in(part_keys[8], 1), 0, V - 1).astype(jnp.int32)
    return {"frame_enc": frame_enc, "phrase_enc": phrase_enc, "key_weight": key_weight, "out_weight": out_weight, "gate_weight": gate_weight, "phrase_token": phrase_token, "bias_blocks": bias_blocks, "utt_lengths": utt_lengths, "targets": targets}


score_gain = 2.0
masked_low = -1e+30

def reference(frame_enc, phrase_enc, key_weight, out_weight, gate_weight, phrase_token, bias_blocks, utt_lengths, targets):
    phrase_keys = jnp.dot(phrase_enc, key_weight, preferred_element_type=jnp.float32).astype(jnp.bfloat16)
    key_blocks = phrase_keys.reshape(BLOCKS, BLK, J)
    token_blocks = phrase_token.reshape(BLOCKS, BLK)
    frame_packs = frame_enc.reshape(PACKS, FR_DEV, J)
    target_packs = targets.reshape(PACKS, FR_DEV)
    owner_utt = jnp.repeat(jnp.arange(ENTRIES, dtype=jnp.int32) // LIST, BLK)
    scale = score_gain / math.sqrt(J)

    def pack_loss(inputs_pack):
        frame_rows, target_row, list_row, lengths_row = inputs_pack
        slot_keys = jnp.take(key_blocks, list_row, axis=0).reshape(ENTRIES * BLK, J)
        slot_token = jnp.take(token_blocks, list_row, axis=0).reshape(ENTRIES * BLK)
        utt_ends = jnp.cumsum(lengths_row, dtype=jnp.int32)
        frame_utt = lax.optimization_barrier(jnp.sum(jnp.arange(FR_DEV, dtype=jnp.int32)[:, None] >= utt_ends[None, :], axis=1, dtype=jnp.int32))
        scores = jnp.dot(frame_rows, slot_keys.T, preferred_element_type=jnp.float32) * scale
        visible = frame_utt[:, None] == owner_utt[None, :]
        target_hit = visible & (slot_token[None, :] == target_row[:, None])
        masked = jnp.where(visible, scores, masked_low)
        row_top = lax.optimization_barrier(jnp.max(masked, axis=1))
        row_exp = jnp.where(visible, jnp.exp(masked - row_top[:, None]), 0.0)
        row_total = lax.optimization_barrier(jnp.sum(row_exp, axis=1))
        pointer = lax.optimization_barrier(jnp.sum(jnp.where(target_hit, row_exp, 0.0), axis=1))
        weights = (row_exp / row_total[:, None]).astype(jnp.bfloat16)
        context = jnp.dot(weights, slot_keys, preferred_element_type=jnp.float32)
        hidden = jnp.tanh(frame_rows.astype(jnp.float32) + context).astype(jnp.bfloat16)
        gate_prob = jax.nn.sigmoid(lax.optimization_barrier(jnp.sum(hidden.astype(jnp.float32) * gate_weight[None, :], axis=1)))
        logits = jnp.dot(hidden, out_weight, preferred_element_type=jnp.float32)
        vocab_top = lax.optimization_barrier(jnp.max(logits, axis=1))
        log_norm = vocab_top + jnp.log(lax.optimization_barrier(jnp.sum(jnp.exp(logits - vocab_top[:, None]), axis=1)))
        target_logit = jnp.take_along_axis(logits, target_row[:, None], axis=1)[:, 0]
        mixed = (1.0 - gate_prob) * jnp.exp(target_logit - log_norm) + gate_prob * (pointer / row_total)
        return -jnp.log(mixed)
    losses = lax.map(pack_loss, (frame_packs, target_packs, bias_blocks, utt_lengths))
    return losses.reshape(FRAMES)
```

```python
import functools
import math

import jax
import jax.numpy as jnp
from jax import lax
from jax.experimental import pallas as pl
from jax.experimental.pallas import tpu as pltpu
from jax.sharding import PartitionSpec as P

BLK = 64
MESH = pl.DeviceIdType.MESH
GAIN = 2.0
HIDDEN_LOW = -1e30
FLOOR = -1e25
F32 = jnp.float32
BF16 = jnp.bfloat16
PIECES = 2
ROWS = 256


def eye(n):
    return lax.broadcasted_iota(jnp.int32, (n, n), 0) == lax.broadcasted_iota(jnp.int32, (n, n), 1)


def to_row(col):
    return jnp.sum(jnp.where(eye(col.shape[0]), col, 0.0), axis=0, keepdims=True)


def to_col(row):
    return jnp.sum(jnp.where(eye(row.shape[1]), row, 0.0), axis=1, keepdims=True)


def lane_sum(x):
    total = x[:, :128]
    for i in range(1, x.shape[1] // 128):
        total = total + x[:, i * 128 : (i + 1) * 128]
    return total


def kernel(
    dims,
    frame_hbm, phrase_hbm, kw_hbm, ow_hbm, gw_ref, tok_ref, list_ref, utt_ref, tgt_ref,
    out_ref,
    frames, phrase, kw, keys, ow_all, tcol, bcol, m_ref, l_ref, p_ref, acc,
    c1_send, c1_recv, s1_send, s1_recv, c2_send, c2_recv, s2_send, s2_recv, hid, st3,
    load_sem, rs, rr, ls, lr, ow_s, ow_r, x1_s, x1_r, x2_s, x2_r, h_s, h_r, t_s, t_r,
):
    packs, mp, sub, lanes = dims
    z, x, c = lax.axis_index("pack"), lax.axis_index("mp"), lax.axis_index("sub")
    plane = mp * sub
    me = x * sub + c
    other = 1 - c
    fr, width = frames.shape
    own_half = phrase.shape[0]
    ph = own_half // PIECES
    half = fr // sub
    part = half // mp
    vcols = ow_hbm.shape[1]
    utts = utt_ref.shape[1]
    entries = list_ref.shape[1]
    per_utt = entries // utts
    half_blocks = own_half // BLK
    scale = GAIN / math.sqrt(width)

    barrier = pltpu.get_barrier_semaphore()

    @pl.when(z > 0)
    def _():
        pl.semaphore_signal(barrier, inc=1, device_id={"pack": z - 1}, device_id_type=MESH)

    @pl.when(z + 1 < packs)
    def _():
        pl.semaphore_signal(barrier, inc=1, device_id={"pack": z + 1}, device_id_type=MESH)

    def peer(j):
        d = lax.rem(me + j, plane)
        return {"mp": d // sub, "sub": lax.rem(d, sub)}

    for j in range(1, plane):
        pl.semaphore_signal(barrier, inc=1, device_id=peer(j), device_id_type=MESH)

    loads = [
        pltpu.make_async_copy(phrase_hbm.at[pl.ds(c * own_half, own_half), :], phrase, load_sem.at[0]),
        pltpu.make_async_copy(kw_hbm, kw, load_sem.at[1]),
        pltpu.make_async_copy(frame_hbm, frames, load_sem.at[2]),
        pltpu.make_async_copy(ow_hbm, ow_all.at[x], load_sem.at[3]),
    ]
    for load in loads:
        load.start()

    def right(s, origin):
        piece = keys.at[origin, pl.ds(lax.rem(s, PIECES) * ph, ph), :]
        return pltpu.make_async_remote_copy(
            src_ref=piece, dst_ref=piece, send_sem=rs.at[s], recv_sem=rr.at[s],
            device_id={"pack": lax.min(z + 1, packs - 1)}, device_id_type=MESH,
        )

    def left(s, origin):
        piece = keys.at[origin, pl.ds(lax.rem(s, PIECES) * ph, ph), :]
        return pltpu.make_async_remote_copy(
            src_ref=piece, dst_ref=piece, send_sem=ls.at[s], recv_sem=lr.at[s],
            device_id={"pack": lax.max(z - 1, 0)}, device_id_type=MESH,
        )

    loads[0].wait()
    loads[1].wait()
    ends_n = jnp.where(z > 0, 1, 0) + jnp.where(z + 1 < packs, 1, 0)
    pl.semaphore_wait(barrier, ends_n + (plane - 1))

    def project(h, carry):
        rows = pl.ds(h * ph, ph)
        keys[z, rows, :] = jnp.dot(phrase[rows, :], kw[...], preferred_element_type=F32).astype(BF16)

        @pl.when(z + 1 < packs)
        def _():
            right(h, z).start()

        @pl.when(z > 0)
        def _():
            left(h, z).start()

        return carry

    lax.fori_loop(0, PIECES, project, 0)

    loads[2].wait()
    loads[3].wait()

    def ow_copy(j, slot):
        return pltpu.make_async_remote_copy(
            src_ref=ow_all.at[slot], dst_ref=ow_all.at[slot], send_sem=ow_s.at[j - 1], recv_sem=ow_r.at[j - 1],
            device_id={"mp": lax.rem(x + j, mp)}, device_id_type=MESH,
        )

    for j in range(1, mp):
        ow_copy(j, x).start()

    for i in range(fr // 128):
        tcol[i * 128 : (i + 1) * 128, :] = to_col(tgt_ref[i : i + 1, :].astype(F32))
    bcol[...] = to_col(list_ref[pl.ds(z, 1), :].astype(F32))
    m_ref[...] = jnp.full(m_ref.shape, FLOOR, F32)
    l_ref[...] = jnp.zeros(l_ref.shape, F32)
    p_ref[...] = jnp.zeros(p_ref.shape, F32)
    acc[...] = jnp.zeros(acc.shape, F32)
    ends = []
    so_far = 0
    for u in range(utts):
        so_far = so_far + utt_ref[0, u]
        ends.append(so_far)

    def process(origin, h):
        k = keys[origin, pl.ds(h * ph, ph), :]
        block = (origin * mp + x) * (half_blocks * sub) + c * half_blocks + h * (ph // BLK)
        ids = (block + lax.broadcasted_iota(jnp.int32, (1, ph), 1) // BLK).astype(F32)
        listed = jnp.where(bcol[...] == ids, 1.0, 0.0)
        log_count = []
        for u in range(utts):
            count = jnp.sum(listed[u * per_utt : (u + 1) * per_utt, :], axis=0, keepdims=True)
            log_count.append(jnp.where(count > 0.5, jnp.log(jnp.maximum(count, 1.0)), HIDDEN_LOW))
        tok_first = block * BLK // 128
        tokens = jnp.concatenate(
            [tok_ref[pl.ds(tok_first + i, 1), :] for i in range(ph // 128)], axis=1
        ).astype(F32)

        def rows_step(i, carry):
            rows = pl.ds(i * ROWS, ROWS)
            s = lax.dot_general(frames[rows, :], k, (((1,), (1,)), ((), ())), preferred_element_type=F32)
            frame_id = lax.broadcasted_iota(jnp.int32, (ROWS, ph), 0) + i * ROWS
            bias = jnp.broadcast_to(log_count[utts - 1], (ROWS, ph))
            for u in range(utts - 2, -1, -1):
                bias = jnp.where(frame_id < ends[u], log_count[u], bias)
            s = s * scale + bias
            old = m_ref[rows, :]
            new = jnp.maximum(old, jnp.max(s, axis=1, keepdims=True))
            fade = jnp.exp(old - new)
            e = jnp.exp(s - new)
            hits = jnp.where(tokens == tcol[rows, :], e, 0.0)
            m_ref[rows, :] = new
            l_ref[rows, :] = l_ref[rows, :] * fade + lane_sum(e)
            p_ref[rows, :] = p_ref[rows, :] * fade + lane_sum(hits)
            acc[rows, :] = acc[rows, :] * fade + jnp.dot(e.astype(BF16), k, preferred_element_type=F32)
            return carry

        lax.fori_loop(0, fr // ROWS, rows_step, 0)

    def own_step(h, carry):
        process(z, h)
        return carry

    lax.fori_loop(0, PIECES, own_step, 0)

    def gather_step(s, carry):
        t, h = s // PIECES, lax.rem(s, PIECES)
        from_left, from_right = z - 1 - t, z + 1 + t

        @pl.when(from_left >= 0)
        def _():
            right(s, from_left).wait_recv()

            @pl.when(z + 1 < packs)
            def _():
                right(s + PIECES, from_left).start()

        @pl.when(from_right < packs)
        def _():
            left(s, from_right).wait_recv()

            @pl.when(z > 0)
            def _():
                left(s + PIECES, from_right).start()

        @pl.when(from_left >= 0)
        def _():
            process(from_left, h)

        @pl.when(from_right < packs)
        def _():
            process(from_right, h)

        return carry

    lax.fori_loop(0, (packs - 1) * PIECES, gather_step, 0)

    blocks = half // lanes
    for i in range(blocks):
        rows = pl.ds(other * half + i * lanes, lanes)
        c1_send[i * lanes : (i + 1) * lanes, :] = acc[rows, :].astype(BF16)
        s1_send[0, i : i + 1, :] = to_row(m_ref[rows, :])
        s1_send[1, i : i + 1, :] = to_row(jnp.sum(l_ref[rows, :], axis=1, keepdims=True))
        s1_send[2, i : i + 1, :] = to_row(jnp.sum(p_ref[rows, :], axis=1, keepdims=True))

    def to_other(src, dst, send, recv):
        return pltpu.make_async_remote_copy(
            src_ref=src, dst_ref=dst, send_sem=send, recv_sem=recv,
            device_id={"sub": other}, device_id_type=MESH,
        )

    first = [
        to_other(c1_send, c1_recv, x1_s.at[0], x1_r.at[0]),
        to_other(s1_send, s1_recv, x1_s.at[1], x1_r.at[1]),
    ]
    for copy in first:
        copy.start()
    for copy in first:
        copy.wait_recv()

    def merge(rows, total, pointer, more, stats):
        old = m_ref[rows, :]
        theirs = to_col(stats[0])
        new = jnp.maximum(old, theirs)
        a, b = jnp.exp(old - new), jnp.exp(theirs - new)
        m_ref[rows, :] = new
        total = total * a + to_col(stats[1]) * b
        pointer = pointer * a + to_col(stats[2]) * b
        acc[rows, :] = acc[rows, :] * a + more.astype(F32) * b
        return total, pointer

    def second(j):
        return [
            pltpu.make_async_remote_copy(
                src_ref=a.at[j - 1], dst_ref=b.at[j - 1],
                send_sem=x2_s.at[2 * (j - 1) + k], recv_sem=x2_r.at[2 * (j - 1) + k],
                device_id={"mp": lax.rem(x + j, mp)}, device_id_type=MESH,
            )
            for k, (a, b) in enumerate(((c2_send, c2_recv), (s2_send, s2_recv)))
        ]

    per = part // lanes
    own_totals = []
    for j in list(range(1, mp)) + [0]:
        target = lax.rem(x + j, mp)
        for i in range(per):
            at = target * part + i * lanes
            rows = pl.ds(c * half + at, lanes)
            spot = target * per + i
            total, pointer = merge(
                rows,
                jnp.sum(l_ref[rows, :], axis=1, keepdims=True),
                jnp.sum(p_ref[rows, :], axis=1, keepdims=True),
                c1_recv[pl.ds(at, lanes), :],
                [s1_recv[k, pl.ds(spot, 1), :] for k in range(3)],
            )
            if j == 0:
                own_totals.append((total, pointer))
            else:
                c2_send[j - 1, i * lanes : (i + 1) * lanes, :] = acc[rows, :].astype(BF16)
                s2_send[j - 1, 0, i : i + 1, :] = to_row(m_ref[rows, :])
                s2_send[j - 1, 1, i : i + 1, :] = to_row(total)
                s2_send[j - 1, 2, i : i + 1, :] = to_row(pointer)
        if j > 0:
            for copy in second(j):
                copy.start()
    for j in range(1, mp):
        for copy in second(j):
            copy.wait_recv()
    own_first = c * half + x * part
    for i in range(per):
        rows = pl.ds(own_first + i * lanes, lanes)
        total, pointer = own_totals[i]
        for j in range(1, mp):
            total, pointer = merge(
                rows, total, pointer,
                c2_recv[j - 1, i * lanes : (i + 1) * lanes, :],
                [s2_recv[j - 1, k, i : i + 1, :] for k in range(3)],
            )
        hidden = jnp.tanh(frames[rows, :].astype(F32) + acc[rows, :] / total).astype(BF16)
        hid[pl.ds(c * part + i * lanes, lanes), :] = hidden
        gate = jnp.sum(hidden.astype(F32) * gw_ref[...], axis=1, keepdims=True)
        st3[me, 3 * sub, i : i + 1, :] = to_row(gate)
        st3[me, 3 * sub + 1, i : i + 1, :] = to_row(pointer / total)

    mine = hid.at[pl.ds(c * part, part), :]
    hid_copy = to_other(mine, mine, h_s, h_r)
    hid_copy.start()
    for j in range(1, mp):
        ow_copy(j, lax.rem(x + mp - j, mp)).wait_recv()

    chunk = min(512, vcols)

    def vocabulary(g):
        h = hid[pl.ds(g * part, part), :]
        target = tcol[pl.ds(g * half + x * part, part), :]
        top = jnp.full((part, 128), FLOOR, F32)
        total = jnp.zeros((part, 128), F32)
        chosen = jnp.zeros((part, 128), F32)
        for q in range(mp):
            for v in range(vcols // chunk):
                w = ow_all[q, :, v * chunk : (v + 1) * chunk]
                logits = jnp.dot(h, w, preferred_element_type=F32)
                first_col = (q * sub + c) * vcols + v * chunk
                ids = (lax.broadcasted_iota(jnp.int32, (1, chunk), 1) + first_col).astype(F32)
                chosen = chosen + lane_sum(jnp.where(ids == target, logits, 0.0))
                new = top
                for i in range(chunk // 128):
                    new = jnp.maximum(new, logits[:, i * 128 : (i + 1) * 128])
                total = total * jnp.exp(top - new)
                for i in range(chunk // 128):
                    total = total + jnp.exp(logits[:, i * 128 : (i + 1) * 128] - new)
                top = new
        row_top = jnp.max(top, axis=1, keepdims=True)
        row_sum = jnp.sum(total * jnp.exp(top - row_top), axis=1, keepdims=True)
        row_hit = jnp.sum(chosen, axis=1, keepdims=True)
        for i in range(per):
            cut = slice(i * lanes, (i + 1) * lanes)
            st3[me, g * 3, i : i + 1, :] = to_row(row_top[cut])
            st3[me, g * 3 + 1, i : i + 1, :] = to_row(row_sum[cut])
            st3[me, g * 3 + 2, i : i + 1, :] = to_row(row_hit[cut])

    vocabulary(c)
    to_other(mine, hid.at[pl.ds(other * part, part), :], h_s, h_r).wait_recv()
    vocabulary(other)

    def share(j, slot):
        return pltpu.make_async_remote_copy(
            src_ref=st3.at[slot], dst_ref=st3.at[slot], send_sem=t_s.at[j - 1], recv_sem=t_r.at[j - 1],
            device_id=peer(j), device_id_type=MESH,
        )

    for j in range(1, plane):
        share(j, me).start()
    for j in range(1, plane):
        share(j, lax.rem(me + plane - j, plane)).wait_recv()

    for q in range(mp):
        for g in range(sub):
            one, two = q * sub, q * sub + 1
            top_a, top_b = st3[one, g * 3], st3[two, g * 3]
            top = jnp.maximum(top_a, top_b)
            total = st3[one, g * 3 + 1] * jnp.exp(top_a - top) + st3[two, g * 3 + 1] * jnp.exp(top_b - top)
            log_norm = top + jnp.log(total)
            hit = st3[one, g * 3 + 2] + st3[two, g * 3 + 2]
            gate = 1.0 / (1.0 + jnp.exp(-st3[q * sub + g, 3 * sub]))
            mixed = (1.0 - gate) * jnp.exp(hit - log_norm) + gate * st3[q * sub + g, 3 * sub + 1]
            first_row = (g * mp + q) * per
            out_ref[first_row : first_row + per, :] = -jnp.log(mixed)

    def send_waits(s, carry):
        t = s // PIECES

        @pl.when((z >= t) & (z + 1 < packs))
        def _():
            right(s, z - t).wait_send()

        @pl.when((z + t < packs) & (z > 0))
        def _():
            left(s, z + t).wait_send()

        return carry

    lax.fori_loop(0, (packs - 1) * PIECES, send_waits, 0)
    for copy in first:
        copy.wait_send()
    hid_copy.wait_send()
    for j in range(1, mp):
        ow_copy(j, x).wait_send()
        for copy in second(j):
            copy.wait_send()
    for j in range(1, plane):
        share(j, me).wait_send()


def per_device(
    frame_enc, phrase_enc, key_weight, out_weight, gate_weight,
    phrase_token, bias_blocks, utt_lengths, targets,
):
    packs = lax.axis_size("pack")
    mp = lax.axis_size("mp")
    sub = lax.axis_size("sub")
    plane = mp * sub
    fr, width = frame_enc.shape
    depth = phrase_enc.shape[1]
    own_half = phrase_enc.shape[0] // sub
    vcols = out_weight.shape[1]
    half = fr // sub
    part = half // mp
    lanes = min(part, 128)
    entries = bias_blocks.shape[1]
    hops = (packs - 1) * PIECES
    others = max(mp - 1, 1)
    vmem = pltpu.VMEM
    dma = pltpu.SemaphoreType.DMA
    any_spec = pl.BlockSpec(memory_space=pl.ANY)
    vmem_spec = pl.BlockSpec(memory_space=vmem)
    smem_spec = pl.BlockSpec(memory_space=pltpu.SMEM)
    out = pl.pallas_call(
        functools.partial(kernel, (packs, mp, sub, lanes)),
        out_shape=jax.ShapeDtypeStruct((fr // lanes, lanes), F32),
        in_specs=[any_spec] * 4 + [vmem_spec] * 3 + [smem_spec, vmem_spec],
        out_specs=vmem_spec,
        scratch_shapes=[
            vmem((fr, width), BF16),
            vmem((own_half, depth), BF16),
            vmem((depth, width), BF16),
            vmem((packs, own_half, width), BF16),
            vmem((mp, width, vcols), BF16),
            vmem((fr, 1), F32),
            vmem((entries, 1), F32),
            vmem((fr, 1), F32),
            vmem((fr, 128), F32),
            vmem((fr, 128), F32),
            vmem((fr, width), F32),
            vmem((half, width), BF16),
            vmem((half, width), BF16),
            vmem((3, half // lanes, lanes), F32),
            vmem((3, half // lanes, lanes), F32),
            vmem((others, part, width), BF16),
            vmem((others, part, width), BF16),
            vmem((others, 3, part // lanes, lanes), F32),
            vmem((others, 3, part // lanes, lanes), F32),
            vmem((sub * part, width), BF16),
            vmem((plane, 3 * sub + 2, part // lanes, lanes), F32),
            dma((4,)), dma((hops,)), dma((hops,)), dma((hops,)), dma((hops,)),
            dma((others,)), dma((others,)), dma((2,)), dma((2,)),
            dma((2 * others,)), dma((2 * others,)), dma, dma,
            dma((plane - 1,)), dma((plane - 1,)),
        ],
        compiler_params=pltpu.CompilerParams(
            collective_id=0, has_side_effects=True, vmem_limit_bytes=56 * 1024 * 1024
        ),
    )(
        frame_enc, phrase_enc, key_weight, out_weight,
        gate_weight.reshape(1, width),
        phrase_token.reshape(-1, 128),
        bias_blocks, utt_lengths,
        targets.reshape(-1, 128),
    )
    return out.reshape(fr)


def solution(mesh):
    in_specs = (
        P(("groups", "pack"), None),
        P(("groups", "pack", "mp"), None),
        P(),
        P(None, ("mp", "sub")),
        P(),
        P("groups"),
        P("groups", None),
        P(("groups", "pack"), None),
        P(("groups", "pack")),
    )
    return jax.shard_map(
        per_device, mesh=mesh, in_specs=in_specs, out_specs=P(("groups", "pack")), check_vma=False
    )
```

```python
import functools
import math

import jax
import jax.numpy as jnp
from jax import lax
from jax.experimental import pallas as pl
from jax.experimental.pallas import tpu as pltpu
from jax.sharding import PartitionSpec as P

BLK = 64
MESH = pl.DeviceIdType.MESH
GAIN = 2.0
HIDDEN_LOW = -1e30
FLOOR = -1e25
F32 = jnp.float32
BF16 = jnp.bfloat16
PIECES = 4
ROWS = 256


def eye(n):
    return lax.broadcasted_iota(jnp.int32, (n, n), 0) == lax.broadcasted_iota(jnp.int32, (n, n), 1)


def to_row(col):
    return jnp.sum(jnp.where(eye(col.shape[0]), col, 0.0), axis=0, keepdims=True)


def to_col(row):
    return jnp.sum(jnp.where(eye(row.shape[1]), row, 0.0), axis=1, keepdims=True)


def lane_sum(x):
    total = x[:, :128]
    for i in range(1, x.shape[1] // 128):
        total = total + x[:, i * 128 : (i + 1) * 128]
    return total


def kernel(
    dims,
    frame_hbm, phrase_hbm, kw_hbm, ow_hbm, gw_ref, tok_ref, list_ref, utt_ref, tgt_ref,
    out_ref,
    frames, phrase, kw, keys, ow_all, tcol, bcol, m_ref, l_ref, p_ref, acc,
    c2_send, c2_recv, s2_send, s2_recv, hid, st3,
    load_sem, rs, rr, ls, lr, cs, cr, ow_s, ow_r, x2_s, x2_r, h_s, h_r, t_s, t_r,
):
    packs, mp, sub, lanes = dims
    z, x, c = lax.axis_index("pack"), lax.axis_index("mp"), lax.axis_index("sub")
    plane = mp * sub
    me = x * sub + c
    other = 1 - c
    half, width = frames.shape
    own_half = phrase.shape[0]
    ph = own_half // PIECES
    both = sub * ph
    part = half // mp
    vcols = ow_hbm.shape[1]
    utts = utt_ref.shape[1]
    entries = list_ref.shape[1]
    per_utt = entries // utts
    half_blocks = own_half // BLK
    scale = GAIN / math.sqrt(width)
    per = part // lanes
    step_rows = min(ROWS, part)

    barrier = pltpu.get_barrier_semaphore()

    @pl.when(z > 0)
    def _():
        pl.semaphore_signal(barrier, inc=1, device_id={"pack": z - 1}, device_id_type=MESH)

    @pl.when(z + 1 < packs)
    def _():
        pl.semaphore_signal(barrier, inc=1, device_id={"pack": z + 1}, device_id_type=MESH)

    def peer(j):
        d = lax.rem(me + j, plane)
        return {"mp": d // sub, "sub": lax.rem(d, sub)}

    for j in range(1, plane):
        pl.semaphore_signal(barrier, inc=1, device_id=peer(j), device_id_type=MESH)

    def phrase_load(h):
        return pltpu.make_async_copy(
            phrase_hbm.at[pl.ds(c * own_half + h * ph, ph), :], phrase.at[pl.ds(h * ph, ph), :], load_sem.at[3 + h]
        )

    loads = [
        pltpu.make_async_copy(kw_hbm, kw, load_sem.at[0]),
        pltpu.make_async_copy(frame_hbm.at[pl.ds(c * half, half), :], frames, load_sem.at[1]),
        pltpu.make_async_copy(ow_hbm, ow_all.at[x], load_sem.at[2]),
    ]
    loads[0].start()
    for h in range(PIECES):
        phrase_load(h).start()
    loads[2].start()
    loads[1].start()

    def right(s, origin):
        piece = keys.at[origin, lax.rem(s, PIECES), c]
        return pltpu.make_async_remote_copy(
            src_ref=piece, dst_ref=piece, send_sem=rs.at[s], recv_sem=rr.at[s],
            device_id={"pack": lax.min(z + 1, packs - 1)}, device_id_type=MESH,
        )

    def left(s, origin):
        piece = keys.at[origin, lax.rem(s, PIECES), c]
        return pltpu.make_async_remote_copy(
            src_ref=piece, dst_ref=piece, send_sem=ls.at[s], recv_sem=lr.at[s],
            device_id={"pack": lax.max(z - 1, 0)}, device_id_type=MESH,
        )

    def to_other(src, dst, send, recv):
        return pltpu.make_async_remote_copy(
            src_ref=src, dst_ref=dst, send_sem=send, recv_sem=recv,
            device_id={"sub": other}, device_id_type=MESH,
        )

    def across(origin, h, core):
        piece = keys.at[origin, h, core]
        spot = origin * PIECES + h
        return to_other(piece, piece, cs.at[spot], cr.at[spot])

    ends_n = jnp.where(z > 0, 1, 0) + jnp.where(z + 1 < packs, 1, 0)
    pl.semaphore_wait(barrier, ends_n + (plane - 1))
    loads[0].wait()

    def project(h, carry):
        phrase_load(h).wait()
        rows = pl.ds(h * ph, ph)
        keys[z, h, c] = jnp.dot(phrase[rows, :], kw[...], preferred_element_type=F32).astype(BF16)

        @pl.when(z + 1 < packs)
        def _():
            right(h, z).start()

        @pl.when(z > 0)
        def _():
            left(h, z).start()

        across(z, h, c).start()
        return carry

    lax.fori_loop(0, PIECES, project, 0)

    loads[2].wait()

    def ow_copy(j, slot):
        return pltpu.make_async_remote_copy(
            src_ref=ow_all.at[slot], dst_ref=ow_all.at[slot], send_sem=ow_s.at[j - 1], recv_sem=ow_r.at[j - 1],
            device_id={"mp": lax.rem(x + j, mp)}, device_id_type=MESH,
        )

    for j in range(1, mp):
        ow_copy(j, x).start()

    loads[1].wait()
    for i in range(sub * half // 128):
        tcol[i * 128 : (i + 1) * 128, :] = to_col(tgt_ref[i : i + 1, :].astype(F32))
    bcol[...] = to_col(list_ref[pl.ds(z, 1), :].astype(F32))
    m_ref[...] = jnp.full(m_ref.shape, FLOOR, F32)
    l_ref[...] = jnp.zeros(l_ref.shape, F32)
    p_ref[...] = jnp.zeros(p_ref.shape, F32)
    acc[...] = jnp.zeros(acc.shape, F32)
    ends = []
    so_far = 0
    for u in range(utts):
        so_far = so_far + utt_ref[0, u]
        ends.append(so_far)

    def process(origin, h):
        across(origin, h, other).wait_recv()
        k = keys[origin, h].reshape(both, width)
        shard = (origin * mp + x) * (half_blocks * sub)
        place = lax.broadcasted_iota(jnp.int32, (1, both), 1)
        ids = shard + (place // ph) * half_blocks + h * (ph // BLK) + lax.rem(place, ph) // BLK
        listed = jnp.where(bcol[...] == ids.astype(F32), 1.0, 0.0)
        log_count = []
        for u in range(utts):
            count = jnp.sum(listed[u * per_utt : (u + 1) * per_utt, :], axis=0, keepdims=True)
            log_count.append(jnp.where(count > 0.5, jnp.log(jnp.maximum(count, 1.0)), HIDDEN_LOW))
        tok_first = shard * BLK // 128 + h * (ph // 128)
        tokens = jnp.concatenate(
            [
                tok_ref[pl.ds(tok_first + core * (own_half // 128) + i, 1), :]
                for core in range(sub)
                for i in range(ph // 128)
            ],
            axis=1,
        ).astype(F32)

        def rows_step(i, carry):
            rows = pl.ds(i * step_rows, step_rows)
            first = c * half + i * step_rows
            s = lax.dot_general(frames[rows, :], k, (((1,), (1,)), ((), ())), preferred_element_type=F32)
            frame_id = lax.broadcasted_iota(jnp.int32, (step_rows, both), 0) + first
            bias = jnp.broadcast_to(log_count[utts - 1], (step_rows, both))
            for u in range(utts - 2, -1, -1):
                bias = jnp.where(frame_id < ends[u], log_count[u], bias)
            s = s * scale + bias
            old = m_ref[rows, :]
            new = jnp.maximum(old, jnp.max(s, axis=1, keepdims=True))
            fade = jnp.exp(old - new)
            e = jnp.exp(s - new)
            hits = jnp.where(tokens == tcol[pl.ds(first, step_rows), :], e, 0.0)
            m_ref[rows, :] = new
            l_ref[rows, :] = l_ref[rows, :] * fade + lane_sum(e)
            p_ref[rows, :] = p_ref[rows, :] * fade + lane_sum(hits)
            acc[rows, :] = acc[rows, :] * fade + jnp.dot(e.astype(BF16), k, preferred_element_type=F32)
            return carry

        lax.fori_loop(0, half // step_rows, rows_step, 0)

    def own_step(h, carry):
        process(z, h)
        return carry

    lax.fori_loop(0, PIECES, own_step, 0)

    def gather_step(s, carry):
        t, h = s // PIECES, lax.rem(s, PIECES)
        from_left, from_right = z - 1 - t, z + 1 + t

        @pl.when(from_left >= 0)
        def _():
            right(s, from_left).wait_recv()

            @pl.when(z + 1 < packs)
            def _():
                right(s + PIECES, from_left).start()

            across(from_left, h, c).start()

        @pl.when(from_right < packs)
        def _():
            left(s, from_right).wait_recv()

            @pl.when(z > 0)
            def _():
                left(s + PIECES, from_right).start()

            across(from_right, h, c).start()

        @pl.when(from_left >= 0)
        def _():
            process(from_left, h)

        @pl.when(from_right < packs)
        def _():
            process(from_right, h)

        return carry

    lax.fori_loop(0, (packs - 1) * PIECES, gather_step, 0)

    def sums(rows):
        return (
            jnp.sum(l_ref[rows, :], axis=1, keepdims=True),
            jnp.sum(p_ref[rows, :], axis=1, keepdims=True),
        )

    def move(j, i):
        src = s2_send.at[j - 1] if i == per else c2_send.at[j - 1, pl.ds(i * lanes, lanes), :]
        dst = s2_recv.at[j - 1] if i == per else c2_recv.at[j - 1, pl.ds(i * lanes, lanes), :]
        spot = (j - 1) * (per + 1) + i
        return pltpu.make_async_remote_copy(
            src_ref=src, dst_ref=dst, send_sem=x2_s.at[spot], recv_sem=x2_r.at[spot],
            device_id={"mp": lax.rem(x + j, mp)}, device_id_type=MESH,
        )

    for j in range(1, mp):
        target = lax.rem(x + j, mp)
        for i in range(per):
            rows = pl.ds(target * part + i * lanes, lanes)
            c2_send[j - 1, i * lanes : (i + 1) * lanes, :] = acc[rows, :].astype(BF16)
            move(j, i).start()
            if i == 0:
                for b in range(per):
                    cut = pl.ds(target * part + b * lanes, lanes)
                    total, pointer = sums(cut)
                    s2_send[j - 1, 0, b : b + 1, :] = to_row(m_ref[cut, :])
                    s2_send[j - 1, 1, b : b + 1, :] = to_row(total)
                    s2_send[j - 1, 2, b : b + 1, :] = to_row(pointer)
                move(j, per).start()

    chunk = min(512, vcols)

    def vocabulary(g, i):
        h = hid[pl.ds(g * part + i * lanes, lanes), :]
        target = tcol[pl.ds(g * half + x * part + i * lanes, lanes), :]
        top = jnp.full((lanes, 128), FLOOR, F32)
        total = jnp.zeros((lanes, 128), F32)
        chosen = jnp.zeros((lanes, 128), F32)
        for q in range(mp):
            for v in range(vcols // chunk):
                w = ow_all[q, :, v * chunk : (v + 1) * chunk]
                logits = jnp.dot(h, w, preferred_element_type=F32)
                first_col = (q * sub + c) * vcols + v * chunk
                ids = (lax.broadcasted_iota(jnp.int32, (1, chunk), 1) + first_col).astype(F32)
                chosen = chosen + lane_sum(jnp.where(ids == target, logits, 0.0))
                new = top
                for b in range(chunk // 128):
                    new = jnp.maximum(new, logits[:, b * 128 : (b + 1) * 128])
                total = total * jnp.exp(top - new)
                for b in range(chunk // 128):
                    total = total + jnp.exp(logits[:, b * 128 : (b + 1) * 128] - new)
                top = new
        row_top = jnp.max(top, axis=1, keepdims=True)
        row_sum = jnp.sum(total * jnp.exp(top - row_top), axis=1, keepdims=True)
        row_hit = jnp.sum(chosen, axis=1, keepdims=True)
        st3[me, g * 3, i : i + 1, :] = to_row(row_top)
        st3[me, g * 3 + 1, i : i + 1, :] = to_row(row_sum)
        st3[me, g * 3 + 2, i : i + 1, :] = to_row(row_hit)

    def hid_copy(i, core):
        block = hid.at[pl.ds(core * part + i * lanes, lanes), :]
        return to_other(block, block, h_s.at[i], h_r.at[i])

    own_sums = [sums(pl.ds(x * part + i * lanes, lanes)) for i in range(per)]
    for j in range(1, mp):
        ow_copy(j, lax.rem(x + mp - j, mp)).wait_recv()
    for j in range(1, mp):
        move(j, per).wait_recv()
    for i in range(per):
        rows = pl.ds(x * part + i * lanes, lanes)
        total, pointer = own_sums[i]
        top = m_ref[rows, :]
        context = acc[rows, :]
        for j in range(1, mp):
            theirs, their_total, their_pointer = [to_col(s2_recv[j - 1, k, i : i + 1, :]) for k in range(3)]
            new = jnp.maximum(top, theirs)
            a, b = jnp.exp(top - new), jnp.exp(theirs - new)
            top = new
            total = total * a + their_total * b
            pointer = pointer * a + their_pointer * b
            move(j, i).wait_recv()
            context = context * a + c2_recv[j - 1, i * lanes : (i + 1) * lanes, :].astype(F32) * b
        hidden = jnp.tanh(frames[rows, :].astype(F32) + context / total).astype(BF16)
        hid[pl.ds(c * part + i * lanes, lanes), :] = hidden
        hid_copy(i, c).start()
        gate = jnp.sum(hidden.astype(F32) * gw_ref[...], axis=1, keepdims=True)
        st3[me, 3 * sub, i : i + 1, :] = to_row(gate)
        st3[me, 3 * sub + 1, i : i + 1, :] = to_row(pointer / total)
        vocabulary(c, i)
        hid_copy(i, other).wait_recv()
        vocabulary(other, i)

    def share(j, slot):
        return pltpu.make_async_remote_copy(
            src_ref=st3.at[slot], dst_ref=st3.at[slot], send_sem=t_s.at[j - 1], recv_sem=t_r.at[j - 1],
            device_id=peer(j), device_id_type=MESH,
        )

    for j in range(1, plane):
        share(j, me).start()
    for j in range(1, plane):
        share(j, lax.rem(me + plane - j, plane)).wait_recv()

    for q in range(mp):
        for g in range(sub):
            one, two = q * sub, q * sub + 1
            top_a, top_b = st3[one, g * 3], st3[two, g * 3]
            top = jnp.maximum(top_a, top_b)
            total = st3[one, g * 3 + 1] * jnp.exp(top_a - top) + st3[two, g * 3 + 1] * jnp.exp(top_b - top)
            log_norm = top + jnp.log(total)
            hit = st3[one, g * 3 + 2] + st3[two, g * 3 + 2]
            gate = 1.0 / (1.0 + jnp.exp(-st3[q * sub + g, 3 * sub]))
            mixed = (1.0 - gate) * jnp.exp(hit - log_norm) + gate * st3[q * sub + g, 3 * sub + 1]
            first_row = (g * mp + q) * per
            out_ref[first_row : first_row + per, :] = -jnp.log(mixed)

    def send_waits(s, carry):
        t = s // PIECES

        @pl.when((z >= t) & (z + 1 < packs))
        def _():
            right(s, z - t).wait_send()

        @pl.when((z + t < packs) & (z > 0))
        def _():
            left(s, z + t).wait_send()

        return carry

    lax.fori_loop(0, (packs - 1) * PIECES, send_waits, 0)

    def core_waits(s, carry):
        across(s // PIECES, lax.rem(s, PIECES), c).wait_send()
        return carry

    lax.fori_loop(0, packs * PIECES, core_waits, 0)
    for i in range(per):
        hid_copy(i, c).wait_send()
    for j in range(1, mp):
        ow_copy(j, x).wait_send()
        for i in range(per + 1):
            move(j, i).wait_send()
    for j in range(1, plane):
        share(j, me).wait_send()


def per_device(
    frame_enc, phrase_enc, key_weight, out_weight, gate_weight,
    phrase_token, bias_blocks, utt_lengths, targets,
):
    packs = lax.axis_size("pack")
    mp = lax.axis_size("mp")
    sub = lax.axis_size("sub")
    plane = mp * sub
    fr, width = frame_enc.shape
    depth = phrase_enc.shape[1]
    own_half = phrase_enc.shape[0] // sub
    vcols = out_weight.shape[1]
    half = fr // sub
    part = half // mp
    lanes = min(part, 128)
    entries = bias_blocks.shape[1]
    hops = (packs - 1) * PIECES
    others = max(mp - 1, 1)
    vmem = pltpu.VMEM
    dma = pltpu.SemaphoreType.DMA
    any_spec = pl.BlockSpec(memory_space=pl.ANY)
    vmem_spec = pl.BlockSpec(memory_space=vmem)
    smem_spec = pl.BlockSpec(memory_space=pltpu.SMEM)
    out = pl.pallas_call(
        functools.partial(kernel, (packs, mp, sub, lanes)),
        out_shape=jax.ShapeDtypeStruct((fr // lanes, lanes), F32),
        in_specs=[any_spec] * 4 + [vmem_spec] * 3 + [smem_spec, vmem_spec],
        out_specs=vmem_spec,
        scratch_shapes=[
            vmem((half, width), BF16),
            vmem((own_half, depth), BF16),
            vmem((depth, width), BF16),
            vmem((packs, PIECES, sub, own_half // PIECES, width), BF16),
            vmem((mp, width, vcols), BF16),
            vmem((fr, 1), F32),
            vmem((entries, 1), F32),
            vmem((half, 1), F32),
            vmem((half, 128), F32),
            vmem((half, 128), F32),
            vmem((half, width), F32),
            vmem((others, part, width), BF16),
            vmem((others, part, width), BF16),
            vmem((others, 3, part // lanes, lanes), F32),
            vmem((others, 3, part // lanes, lanes), F32),
            vmem((sub * part, width), BF16),
            vmem((plane, 3 * sub + 2, part // lanes, lanes), F32),
            dma((3 + PIECES,)), dma((hops,)), dma((hops,)), dma((hops,)), dma((hops,)),
            dma((packs * PIECES,)), dma((packs * PIECES,)),
            dma((others,)), dma((others,)),
            dma((others * (part // lanes + 1),)), dma((others * (part // lanes + 1),)),
            dma((part // lanes,)), dma((part // lanes,)),
            dma((plane - 1,)), dma((plane - 1,)),
        ],
        compiler_params=pltpu.CompilerParams(
            collective_id=0, has_side_effects=True, vmem_limit_bytes=56 * 1024 * 1024
        ),
    )(
        frame_enc, phrase_enc, key_weight, out_weight,
        gate_weight.reshape(1, width),
        phrase_token.reshape(-1, 128),
        bias_blocks, utt_lengths,
        targets.reshape(-1, 128),
    )
    return out.reshape(fr)


def solution(mesh):
    in_specs = (
        P(("groups", "pack"), None),
        P(("groups", "pack", "mp"), None),
        P(),
        P(None, ("mp", "sub")),
        P(),
        P("groups"),
        P("groups", None),
        P(("groups", "pack"), None),
        P(("groups", "pack")),
    )
    return jax.shard_map(
        per_device, mesh=mesh, in_specs=in_specs, out_specs=P(("groups", "pack")), check_vma=False
    )
```

```python
import functools
import math

import jax
import jax.numpy as jnp
from jax import lax
from jax.experimental import pallas as pl
from jax.experimental.pallas import tpu as pltpu
from jax.sharding import PartitionSpec as P

BLK = 64
MESH = pl.DeviceIdType.MESH
GAIN = 2.0
HIDDEN_LOW = -1e30
FLOOR = -1e25
F32 = jnp.float32
BF16 = jnp.bfloat16
PIECES = 4
ROWS = 256


def eye(n):
    return lax.broadcasted_iota(jnp.int32, (n, n), 0) == lax.broadcasted_iota(jnp.int32, (n, n), 1)


def to_row(col):
    return jnp.sum(jnp.where(eye(col.shape[0]), col, 0.0), axis=0, keepdims=True)


def to_col(row):
    return jnp.sum(jnp.where(eye(row.shape[1]), row, 0.0), axis=1, keepdims=True)


def lane_sum(x):
    total = x[:, :128]
    for i in range(1, x.shape[1] // 128):
        total = total + x[:, i * 128 : (i + 1) * 128]
    return total


def kernel(
    dims,
    frame_hbm, phrase_hbm, kw_hbm, ow_hbm, gw_ref, tok_ref, list_ref, utt_ref, tgt_ref,
    out_ref,
    frames, phrase, kw, keys, ow_all, tcol, bcol, log_count, tokens, m_ref, l_ref, p_ref, acc,
    c2_send, c2_recv, s2_send, s2_recv, hid, st3,
    load_sem, rs, rr, ls, lr, cs, cr, ow_s, ow_r, x2_s, x2_r, h_s, h_r, t_s, t_r,
):
    packs, mp, sub, lanes = dims
    z, x, c = lax.axis_index("pack"), lax.axis_index("mp"), lax.axis_index("sub")
    plane = mp * sub
    me = x * sub + c
    other = 1 - c
    half, width = frames.shape
    own_half = phrase.shape[0]
    ph = own_half // PIECES
    both = sub * ph
    part = half // mp
    vcols = ow_hbm.shape[1]
    utts = utt_ref.shape[1]
    entries = list_ref.shape[1]
    per_utt = entries // utts
    half_blocks = own_half // BLK
    scale = GAIN / math.sqrt(width)
    per = part // lanes
    step_rows = min(ROWS, part)

    barrier = pltpu.get_barrier_semaphore()

    @pl.when(z > 0)
    def _():
        pl.semaphore_signal(barrier, inc=1, device_id={"pack": z - 1}, device_id_type=MESH)

    @pl.when(z + 1 < packs)
    def _():
        pl.semaphore_signal(barrier, inc=1, device_id={"pack": z + 1}, device_id_type=MESH)

    def peer(j):
        d = lax.rem(me + j, plane)
        return {"mp": d // sub, "sub": lax.rem(d, sub)}

    for j in range(1, plane):
        pl.semaphore_signal(barrier, inc=1, device_id=peer(j), device_id_type=MESH)

    def phrase_load(h):
        return pltpu.make_async_copy(
            phrase_hbm.at[pl.ds(c * own_half + h * ph, ph), :], phrase.at[pl.ds(h * ph, ph), :], load_sem.at[3 + h]
        )

    loads = [
        pltpu.make_async_copy(kw_hbm, kw, load_sem.at[0]),
        pltpu.make_async_copy(frame_hbm.at[pl.ds(c * half, half), :], frames, load_sem.at[1]),
        pltpu.make_async_copy(ow_hbm, ow_all.at[x], load_sem.at[2]),
    ]
    loads[0].start()
    for h in range(PIECES):
        phrase_load(h).start()
    loads[2].start()
    loads[1].start()

    def right(s, origin):
        piece = keys.at[origin, lax.rem(s, PIECES), c]
        return pltpu.make_async_remote_copy(
            src_ref=piece, dst_ref=piece, send_sem=rs.at[s], recv_sem=rr.at[s],
            device_id={"pack": lax.min(z + 1, packs - 1)}, device_id_type=MESH,
        )

    def left(s, origin):
        piece = keys.at[origin, lax.rem(s, PIECES), c]
        return pltpu.make_async_remote_copy(
            src_ref=piece, dst_ref=piece, send_sem=ls.at[s], recv_sem=lr.at[s],
            device_id={"pack": lax.max(z - 1, 0)}, device_id_type=MESH,
        )

    def to_other(src, dst, send, recv):
        return pltpu.make_async_remote_copy(
            src_ref=src, dst_ref=dst, send_sem=send, recv_sem=recv,
            device_id={"sub": other}, device_id_type=MESH,
        )

    def across(origin, h, core):
        piece = keys.at[origin, h, core]
        spot = origin * PIECES + h
        return to_other(piece, piece, cs.at[spot], cr.at[spot])

    ends_n = jnp.where(z > 0, 1, 0) + jnp.where(z + 1 < packs, 1, 0)
    pl.semaphore_wait(barrier, ends_n + (plane - 1))
    loads[0].wait()

    def project(h, carry):
        phrase_load(h).wait()
        rows = pl.ds(h * ph, ph)
        keys[z, h, c] = jnp.dot(phrase[rows, :], kw[...], preferred_element_type=F32).astype(BF16)

        @pl.when(z + 1 < packs)
        def _():
            right(h, z).start()

        @pl.when(z > 0)
        def _():
            left(h, z).start()

        across(z, h, c).start()
        return carry

    lax.fori_loop(0, PIECES, project, 0)

    loads[2].wait()

    def ow_copy(j, slot):
        return pltpu.make_async_remote_copy(
            src_ref=ow_all.at[slot], dst_ref=ow_all.at[slot], send_sem=ow_s.at[j - 1], recv_sem=ow_r.at[j - 1],
            device_id={"mp": lax.rem(x + j, mp)}, device_id_type=MESH,
        )

    for j in range(1, mp):
        ow_copy(j, x).start()

    loads[1].wait()
    for i in range(sub * half // 128):
        tcol[i * 128 : (i + 1) * 128, :] = to_col(tgt_ref[i : i + 1, :].astype(F32))
    bcol[...] = to_col(list_ref[pl.ds(z, 1), :].astype(F32))
    m_ref[...] = jnp.full(m_ref.shape, FLOOR, F32)
    l_ref[...] = jnp.zeros(l_ref.shape, F32)
    p_ref[...] = jnp.zeros(p_ref.shape, F32)
    acc[...] = jnp.zeros(acc.shape, F32)
    ends = []
    so_far = 0
    for u in range(utts):
        so_far = so_far + utt_ref[0, u]
        ends.append(so_far)

    owner = (
        lax.broadcasted_iota(jnp.int32, (8, entries), 1) // per_utt
        == lax.broadcasted_iota(jnp.int32, (8, entries), 0)
    )
    owner = jnp.where(owner, 1.0, 0.0).astype(BF16)

    def table_step(spot, carry):
        origin, h = spot // PIECES, lax.rem(spot, PIECES)
        shard = (origin * mp + x) * (half_blocks * sub)
        place = lax.broadcasted_iota(jnp.int32, (1, both), 1)
        ids = shard + (place // ph) * half_blocks + h * (ph // BLK) + lax.rem(place, ph) // BLK
        listed = jnp.where(bcol[...] == ids.astype(F32), 1.0, 0.0).astype(BF16)
        count = jnp.dot(owner, listed, preferred_element_type=F32)
        log_count[spot] = jnp.where(count > 0.5, jnp.log(jnp.maximum(count, 1.0)), HIDDEN_LOW)
        tok_first = shard * BLK // 128 + h * (ph // 128)
        tokens[spot] = jnp.concatenate(
            [
                tok_ref[pl.ds(tok_first + core * (own_half // 128) + i, 1), :]
                for core in range(sub)
                for i in range(ph // 128)
            ],
            axis=1,
        ).astype(F32)
        return carry

    lax.fori_loop(0, packs * PIECES, table_step, 0)

    def process(origin, h):
        across(origin, h, other).wait_recv()
        k = keys[origin, h].reshape(both, width)
        spot = origin * PIECES + h

        def rows_step(i, carry):
            rows = pl.ds(i * step_rows, step_rows)
            first = c * half + i * step_rows
            s = lax.dot_general(frames[rows, :], k, (((1,), (1,)), ((), ())), preferred_element_type=F32)
            frame_id = lax.broadcasted_iota(jnp.int32, (step_rows, both), 0) + first
            bias = jnp.broadcast_to(log_count[spot, utts - 1 : utts, :], (step_rows, both))
            for u in range(utts - 2, -1, -1):
                bias = jnp.where(frame_id < ends[u], log_count[spot, u : u + 1, :], bias)
            s = s * scale + bias
            old = m_ref[rows, :]
            new = jnp.maximum(old, jnp.max(s, axis=1, keepdims=True))
            fade = jnp.exp(old - new)
            e = jnp.exp(s - new)
            hits = jnp.where(tokens[spot] == tcol[pl.ds(first, step_rows), :], e, 0.0)
            m_ref[rows, :] = new
            l_ref[rows, :] = l_ref[rows, :] * fade + lane_sum(e)
            p_ref[rows, :] = p_ref[rows, :] * fade + lane_sum(hits)
            acc[rows, :] = acc[rows, :] * fade + jnp.dot(e.astype(BF16), k, preferred_element_type=F32)
            return carry

        lax.fori_loop(0, half // step_rows, rows_step, 0)

    hops = (packs - 1) * PIECES

    def gather_step(s, carry):
        t = s // PIECES
        from_left, from_right = z - 1 - t, z + 1 + t

        @pl.when((s < hops) & (from_left >= 0))
        def _():
            right(s, from_left).wait_recv()

            @pl.when(z + 1 < packs)
            def _():
                right(s + PIECES, from_left).start()

            across(from_left, lax.rem(s, PIECES), c).start()

        @pl.when((s < hops) & (from_right < packs))
        def _():
            left(s, from_right).wait_recv()

            @pl.when(z > 0)
            def _():
                left(s + PIECES, from_right).start()

            across(from_right, lax.rem(s, PIECES), c).start()

        @pl.when(s < PIECES)
        def _():
            process(z, s)

        before = s - 1
        ago, h = before // PIECES, lax.rem(before, PIECES)

        @pl.when((s > 0) & (z - 1 - ago >= 0))
        def _():
            process(z - 1 - ago, h)

        @pl.when((s > 0) & (z + 1 + ago < packs))
        def _():
            process(z + 1 + ago, h)

        return carry

    lax.fori_loop(0, hops + 1, gather_step, 0)

    def sums(rows):
        return (
            jnp.sum(l_ref[rows, :], axis=1, keepdims=True),
            jnp.sum(p_ref[rows, :], axis=1, keepdims=True),
        )

    def move(j, i):
        src = s2_send.at[j - 1] if i == per else c2_send.at[j - 1, pl.ds(i * lanes, lanes), :]
        dst = s2_recv.at[j - 1] if i == per else c2_recv.at[j - 1, pl.ds(i * lanes, lanes), :]
        spot = (j - 1) * (per + 1) + i
        return pltpu.make_async_remote_copy(
            src_ref=src, dst_ref=dst, send_sem=x2_s.at[spot], recv_sem=x2_r.at[spot],
            device_id={"mp": lax.rem(x + j, mp)}, device_id_type=MESH,
        )

    for j in range(1, mp):
        target = lax.rem(x + j, mp)
        for i in range(per):
            rows = pl.ds(target * part + i * lanes, lanes)
            c2_send[j - 1, i * lanes : (i + 1) * lanes, :] = acc[rows, :].astype(BF16)
            move(j, i).start()
            if i == 0:
                for b in range(per):
                    cut = pl.ds(target * part + b * lanes, lanes)
                    total, pointer = sums(cut)
                    s2_send[j - 1, 0, b : b + 1, :] = to_row(m_ref[cut, :])
                    s2_send[j - 1, 1, b : b + 1, :] = to_row(total)
                    s2_send[j - 1, 2, b : b + 1, :] = to_row(pointer)
                move(j, per).start()

    chunk = min(512, vcols)

    def vocabulary(g, i):
        h = hid[pl.ds(g * part + i * lanes, lanes), :]
        target = tcol[pl.ds(g * half + x * part + i * lanes, lanes), :]
        top = jnp.full((lanes, 128), FLOOR, F32)
        total = jnp.zeros((lanes, 128), F32)
        chosen = jnp.zeros((lanes, 128), F32)
        for q in range(mp):
            for v in range(vcols // chunk):
                w = ow_all[q, :, v * chunk : (v + 1) * chunk]
                logits = jnp.dot(h, w, preferred_element_type=F32)
                first_col = (q * sub + c) * vcols + v * chunk
                ids = (lax.broadcasted_iota(jnp.int32, (1, chunk), 1) + first_col).astype(F32)
                chosen = chosen + lane_sum(jnp.where(ids == target, logits, 0.0))
                new = top
                for b in range(chunk // 128):
                    new = jnp.maximum(new, logits[:, b * 128 : (b + 1) * 128])
                total = total * jnp.exp(top - new)
                for b in range(chunk // 128):
                    total = total + jnp.exp(logits[:, b * 128 : (b + 1) * 128] - new)
                top = new
        row_top = jnp.max(top, axis=1, keepdims=True)
        row_sum = jnp.sum(total * jnp.exp(top - row_top), axis=1, keepdims=True)
        row_hit = jnp.sum(chosen, axis=1, keepdims=True)
        st3[me, g * 3, i : i + 1, :] = to_row(row_top)
        st3[me, g * 3 + 1, i : i + 1, :] = to_row(row_sum)
        st3[me, g * 3 + 2, i : i + 1, :] = to_row(row_hit)

    def hid_copy(i, core):
        block = hid.at[pl.ds(core * part + i * lanes, lanes), :]
        return to_other(block, block, h_s.at[i], h_r.at[i])

    own_sums = [sums(pl.ds(x * part + i * lanes, lanes)) for i in range(per)]
    for j in range(1, mp):
        ow_copy(j, lax.rem(x + mp - j, mp)).wait_recv()
    for j in range(1, mp):
        move(j, per).wait_recv()
    for i in range(per):
        rows = pl.ds(x * part + i * lanes, lanes)
        total, pointer = own_sums[i]
        top = m_ref[rows, :]
        context = acc[rows, :]
        for j in range(1, mp):
            theirs, their_total, their_pointer = [to_col(s2_recv[j - 1, k, i : i + 1, :]) for k in range(3)]
            new = jnp.maximum(top, theirs)
            a, b = jnp.exp(top - new), jnp.exp(theirs - new)
            top = new
            total = total * a + their_total * b
            pointer = pointer * a + their_pointer * b
            move(j, i).wait_recv()
            context = context * a + c2_recv[j - 1, i * lanes : (i + 1) * lanes, :].astype(F32) * b
        hidden = jnp.tanh(frames[rows, :].astype(F32) + context / total).astype(BF16)
        hid[pl.ds(c * part + i * lanes, lanes), :] = hidden
        hid_copy(i, c).start()
        gate = jnp.sum(hidden.astype(F32) * gw_ref[...], axis=1, keepdims=True)
        st3[me, 3 * sub, i : i + 1, :] = to_row(gate)
        st3[me, 3 * sub + 1, i : i + 1, :] = to_row(pointer / total)
        vocabulary(c, i)
        hid_copy(i, other).wait_recv()
        vocabulary(other, i)

    def share(j, slot):
        return pltpu.make_async_remote_copy(
            src_ref=st3.at[slot], dst_ref=st3.at[slot], send_sem=t_s.at[j - 1], recv_sem=t_r.at[j - 1],
            device_id=peer(j), device_id_type=MESH,
        )

    for j in range(1, plane):
        share(j, me).start()
    for j in range(1, plane):
        share(j, lax.rem(me + plane - j, plane)).wait_recv()

    for q in range(mp):
        for g in range(sub):
            one, two = q * sub, q * sub + 1
            top_a, top_b = st3[one, g * 3], st3[two, g * 3]
            top = jnp.maximum(top_a, top_b)
            total = st3[one, g * 3 + 1] * jnp.exp(top_a - top) + st3[two, g * 3 + 1] * jnp.exp(top_b - top)
            log_norm = top + jnp.log(total)
            hit = st3[one, g * 3 + 2] + st3[two, g * 3 + 2]
            gate = 1.0 / (1.0 + jnp.exp(-st3[q * sub + g, 3 * sub]))
            mixed = (1.0 - gate) * jnp.exp(hit - log_norm) + gate * st3[q * sub + g, 3 * sub + 1]
            first_row = (g * mp + q) * per
            out_ref[first_row : first_row + per, :] = -jnp.log(mixed)

    def send_waits(s, carry):
        t = s // PIECES

        @pl.when((z >= t) & (z + 1 < packs))
        def _():
            right(s, z - t).wait_send()

        @pl.when((z + t < packs) & (z > 0))
        def _():
            left(s, z + t).wait_send()

        return carry

    lax.fori_loop(0, (packs - 1) * PIECES, send_waits, 0)

    def core_waits(s, carry):
        across(s // PIECES, lax.rem(s, PIECES), c).wait_send()
        return carry

    lax.fori_loop(0, packs * PIECES, core_waits, 0)
    for i in range(per):
        hid_copy(i, c).wait_send()
    for j in range(1, mp):
        ow_copy(j, x).wait_send()
        for i in range(per + 1):
            move(j, i).wait_send()
    for j in range(1, plane):
        share(j, me).wait_send()


def per_device(
    frame_enc, phrase_enc, key_weight, out_weight, gate_weight,
    phrase_token, bias_blocks, utt_lengths, targets,
):
    packs = lax.axis_size("pack")
    mp = lax.axis_size("mp")
    sub = lax.axis_size("sub")
    plane = mp * sub
    fr, width = frame_enc.shape
    depth = phrase_enc.shape[1]
    own_half = phrase_enc.shape[0] // sub
    vcols = out_weight.shape[1]
    half = fr // sub
    part = half // mp
    lanes = min(part, 128)
    entries = bias_blocks.shape[1]
    hops = (packs - 1) * PIECES
    others = max(mp - 1, 1)
    vmem = pltpu.VMEM
    dma = pltpu.SemaphoreType.DMA
    any_spec = pl.BlockSpec(memory_space=pl.ANY)
    vmem_spec = pl.BlockSpec(memory_space=vmem)
    smem_spec = pl.BlockSpec(memory_space=pltpu.SMEM)
    out = pl.pallas_call(
        functools.partial(kernel, (packs, mp, sub, lanes)),
        out_shape=jax.ShapeDtypeStruct((fr // lanes, lanes), F32),
        in_specs=[any_spec] * 4 + [vmem_spec] * 3 + [smem_spec, vmem_spec],
        out_specs=vmem_spec,
        scratch_shapes=[
            vmem((half, width), BF16),
            vmem((own_half, depth), BF16),
            vmem((depth, width), BF16),
            vmem((packs, PIECES, sub, own_half // PIECES, width), BF16),
            vmem((mp, width, vcols), BF16),
            vmem((fr, 1), F32),
            vmem((entries, 1), F32),
            vmem((packs * PIECES, 8, sub * own_half // PIECES), F32),
            vmem((packs * PIECES, 1, sub * own_half // PIECES), F32),
            vmem((half, 1), F32),
            vmem((half, 128), F32),
            vmem((half, 128), F32),
            vmem((half, width), F32),
            vmem((others, part, width), BF16),
            vmem((others, part, width), BF16),
            vmem((others, 3, part // lanes, lanes), F32),
            vmem((others, 3, part // lanes, lanes), F32),
            vmem((sub * part, width), BF16),
            vmem((plane, 3 * sub + 2, part // lanes, lanes), F32),
            dma((3 + PIECES,)), dma((hops,)), dma((hops,)), dma((hops,)), dma((hops,)),
            dma((packs * PIECES,)), dma((packs * PIECES,)),
            dma((others,)), dma((others,)),
            dma((others * (part // lanes + 1),)), dma((others * (part // lanes + 1),)),
            dma((part // lanes,)), dma((part // lanes,)),
            dma((plane - 1,)), dma((plane - 1,)),
        ],
        compiler_params=pltpu.CompilerParams(
            collective_id=0, has_side_effects=True, vmem_limit_bytes=56 * 1024 * 1024
        ),
    )(
        frame_enc, phrase_enc, key_weight, out_weight,
        gate_weight.reshape(1, width),
        phrase_token.reshape(-1, 128),
        bias_blocks, utt_lengths,
        targets.reshape(-1, 128),
    )
    return out.reshape(fr)


def solution(mesh):
    in_specs = (
        P(("groups", "pack"), None),
        P(("groups", "pack", "mp"), None),
        P(),
        P(None, ("mp", "sub")),
        P(),
        P("groups"),
        P("groups", None),
        P(("groups", "pack"), None),
        P(("groups", "pack")),
    )
    return jax.shard_map(
        per_device, mesh=mesh, in_specs=in_specs, out_specs=P(("groups", "pack")), check_vma=False
    )
```

```python
import functools
import math

import jax
import jax.numpy as jnp
from jax import lax
from jax.experimental import pallas as pl
from jax.experimental.pallas import tpu as pltpu
from jax.sharding import PartitionSpec as P

BLK = 64
MESH = pl.DeviceIdType.MESH
GAIN = 2.0
HIDDEN_LOW = -1e30
FLOOR = -1e25
F32 = jnp.float32
BF16 = jnp.bfloat16
PIECES = 4
ROWS = 512


def eye(n):
    return lax.broadcasted_iota(jnp.int32, (n, n), 0) == lax.broadcasted_iota(jnp.int32, (n, n), 1)


def to_row(col):
    return jnp.sum(jnp.where(eye(col.shape[0]), col, 0.0), axis=0, keepdims=True)


def to_col(row):
    return jnp.sum(jnp.where(eye(row.shape[1]), row, 0.0), axis=1, keepdims=True)


def lane_sum(x):
    total = x[:, :128]
    for i in range(1, x.shape[1] // 128):
        total = total + x[:, i * 128 : (i + 1) * 128]
    return total


def kernel(
    dims,
    frame_hbm, phrase_hbm, kw_hbm, ow_hbm, gw_ref, tok_ref, list_ref, utt_ref, tgt_ref,
    out_ref,
    frames, phrase, kw, keys, ow_all, tcol, bcol, log_count, tokens, m_ref, l_ref, p_ref, acc,
    c2_send, c2_recv, s2_send, s2_recv, hid, st3,
    load_sem, rs, rr, ls, lr, cs, cr, ow_s, ow_r, x2_s, x2_r, h_s, h_r, t_s, t_r,
):
    packs, mp, sub, lanes = dims
    z, x, c = lax.axis_index("pack"), lax.axis_index("mp"), lax.axis_index("sub")
    plane = mp * sub
    me = x * sub + c
    other = 1 - c
    half, width = frames.shape
    own_half = phrase.shape[0]
    ph = own_half // PIECES
    both = sub * ph
    part = half // mp
    vcols = ow_hbm.shape[1]
    utts = utt_ref.shape[1]
    entries = list_ref.shape[1]
    per_utt = entries // utts
    half_blocks = own_half // BLK
    scale = GAIN / math.sqrt(width)
    per = part // lanes
    step_rows = min(ROWS, half)

    barrier = pltpu.get_barrier_semaphore()

    @pl.when(z > 0)
    def _():
        pl.semaphore_signal(barrier, inc=1, device_id={"pack": z - 1}, device_id_type=MESH)

    @pl.when(z + 1 < packs)
    def _():
        pl.semaphore_signal(barrier, inc=1, device_id={"pack": z + 1}, device_id_type=MESH)

    def peer(j):
        d = lax.rem(me + j, plane)
        return {"mp": d // sub, "sub": lax.rem(d, sub)}

    for j in range(1, plane):
        pl.semaphore_signal(barrier, inc=1, device_id=peer(j), device_id_type=MESH)

    def phrase_load(h):
        return pltpu.make_async_copy(
            phrase_hbm.at[pl.ds(c * own_half + h * ph, ph), :], phrase.at[pl.ds(h * ph, ph), :], load_sem.at[3 + h]
        )

    loads = [
        pltpu.make_async_copy(kw_hbm, kw, load_sem.at[0]),
        pltpu.make_async_copy(frame_hbm.at[pl.ds(c * half, half), :], frames, load_sem.at[1]),
        pltpu.make_async_copy(ow_hbm, ow_all.at[x], load_sem.at[2]),
    ]
    loads[0].start()
    for h in range(PIECES):
        phrase_load(h).start()
    loads[2].start()
    loads[1].start()

    def right(s, origin):
        piece = keys.at[origin, lax.rem(s, PIECES), c]
        return pltpu.make_async_remote_copy(
            src_ref=piece, dst_ref=piece, send_sem=rs.at[s], recv_sem=rr.at[s],
            device_id={"pack": lax.min(z + 1, packs - 1)}, device_id_type=MESH,
        )

    def left(s, origin):
        piece = keys.at[origin, lax.rem(s, PIECES), c]
        return pltpu.make_async_remote_copy(
            src_ref=piece, dst_ref=piece, send_sem=ls.at[s], recv_sem=lr.at[s],
            device_id={"pack": lax.max(z - 1, 0)}, device_id_type=MESH,
        )

    def to_other(src, dst, send, recv):
        return pltpu.make_async_remote_copy(
            src_ref=src, dst_ref=dst, send_sem=send, recv_sem=recv,
            device_id={"sub": other}, device_id_type=MESH,
        )

    def across(origin, h, core):
        piece = keys.at[origin, h, core]
        spot = origin * PIECES + h
        return to_other(piece, piece, cs.at[spot], cr.at[spot])

    ends_n = jnp.where(z > 0, 1, 0) + jnp.where(z + 1 < packs, 1, 0)
    pl.semaphore_wait(barrier, ends_n + (plane - 1))
    loads[0].wait()

    def project(h, carry):
        phrase_load(h).wait()
        rows = pl.ds(h * ph, ph)
        keys[z, h, c] = jnp.dot(phrase[rows, :], kw[...], preferred_element_type=F32).astype(BF16)

        @pl.when(z + 1 < packs)
        def _():
            right(h, z).start()

        @pl.when(z > 0)
        def _():
            left(h, z).start()

        across(z, h, c).start()
        return carry

    lax.fori_loop(0, PIECES, project, 0)

    loads[2].wait()

    def ow_copy(j, slot):
        return pltpu.make_async_remote_copy(
            src_ref=ow_all.at[slot], dst_ref=ow_all.at[slot], send_sem=ow_s.at[j - 1], recv_sem=ow_r.at[j - 1],
            device_id={"mp": lax.rem(x + j, mp)}, device_id_type=MESH,
        )

    for j in range(1, mp):
        ow_copy(j, x).start()

    loads[1].wait()
    for i in range(sub * half // 128):
        tcol[i * 128 : (i + 1) * 128, :] = to_col(tgt_ref[i : i + 1, :].astype(F32))
    bcol[...] = to_col(list_ref[pl.ds(z, 1), :].astype(F32))
    m_ref[...] = jnp.full(m_ref.shape, FLOOR, F32)
    l_ref[...] = jnp.zeros(l_ref.shape, F32)
    p_ref[...] = jnp.zeros(p_ref.shape, F32)
    acc[...] = jnp.zeros(acc.shape, F32)
    ends = []
    so_far = 0
    for u in range(utts):
        so_far = so_far + utt_ref[0, u]
        ends.append(so_far)

    owner = (
        lax.broadcasted_iota(jnp.int32, (8, entries), 1) // per_utt
        == lax.broadcasted_iota(jnp.int32, (8, entries), 0)
    )
    owner = jnp.where(owner, 1.0, 0.0).astype(BF16)

    def table_step(spot, carry):
        origin, h = spot // PIECES, lax.rem(spot, PIECES)
        shard = (origin * mp + x) * (half_blocks * sub)
        place = lax.broadcasted_iota(jnp.int32, (1, both), 1)
        ids = shard + (place // ph) * half_blocks + h * (ph // BLK) + lax.rem(place, ph) // BLK
        listed = jnp.where(bcol[...] == ids.astype(F32), 1.0, 0.0).astype(BF16)
        count = jnp.dot(owner, listed, preferred_element_type=F32)
        log_count[spot] = jnp.where(count > 0.5, jnp.log(jnp.maximum(count, 1.0)), HIDDEN_LOW)
        tok_first = shard * BLK // 128 + h * (ph // 128)
        tokens[spot] = jnp.concatenate(
            [
                tok_ref[pl.ds(tok_first + core * (own_half // 128) + i, 1), :]
                for core in range(sub)
                for i in range(ph // 128)
            ],
            axis=1,
        ).astype(F32)
        return carry

    lax.fori_loop(0, packs * PIECES, table_step, 0)

    def process(origin, h):
        across(origin, h, other).wait_recv()
        k = keys[origin, h].reshape(both, width)
        spot = origin * PIECES + h

        def rows_step(i, carry):
            rows = pl.ds(i * step_rows, step_rows)
            first = c * half + i * step_rows
            s = lax.dot_general(frames[rows, :], k, (((1,), (1,)), ((), ())), preferred_element_type=F32)
            frame_id = lax.broadcasted_iota(jnp.int32, (step_rows, both), 0) + first
            bias = jnp.broadcast_to(log_count[spot, utts - 1 : utts, :], (step_rows, both))
            for u in range(utts - 2, -1, -1):
                bias = jnp.where(frame_id < ends[u], log_count[spot, u : u + 1, :], bias)
            s = s * scale + bias
            old = m_ref[rows, :]
            new = jnp.maximum(old, jnp.max(s, axis=1, keepdims=True))
            fade = jnp.exp(old - new)
            e = jnp.exp(s - new)
            hits = jnp.where(tokens[spot] == tcol[pl.ds(first, step_rows), :], e, 0.0)
            m_ref[rows, :] = new
            l_ref[rows, :] = l_ref[rows, :] * fade + lane_sum(e)
            p_ref[rows, :] = p_ref[rows, :] * fade + lane_sum(hits)
            acc[rows, :] = acc[rows, :] * fade + jnp.dot(e.astype(BF16), k, preferred_element_type=F32)
            return carry

        lax.fori_loop(0, half // step_rows, rows_step, 0)

    hops = (packs - 1) * PIECES

    def gather_step(s, carry):
        t = s // PIECES
        from_left, from_right = z - 1 - t, z + 1 + t

        @pl.when((s < hops) & (from_left >= 0))
        def _():
            right(s, from_left).wait_recv()

            @pl.when(z + 1 < packs)
            def _():
                right(s + PIECES, from_left).start()

            across(from_left, lax.rem(s, PIECES), c).start()

        @pl.when((s < hops) & (from_right < packs))
        def _():
            left(s, from_right).wait_recv()

            @pl.when(z > 0)
            def _():
                left(s + PIECES, from_right).start()

            across(from_right, lax.rem(s, PIECES), c).start()

        @pl.when(s < PIECES)
        def _():
            process(z, s)

        before = s - 1
        ago, h = before // PIECES, lax.rem(before, PIECES)

        @pl.when((s > 0) & (z - 1 - ago >= 0))
        def _():
            process(z - 1 - ago, h)

        @pl.when((s > 0) & (z + 1 + ago < packs))
        def _():
            process(z + 1 + ago, h)

        return carry

    lax.fori_loop(0, hops + 1, gather_step, 0)

    def sums(rows):
        return (
            jnp.sum(l_ref[rows, :], axis=1, keepdims=True),
            jnp.sum(p_ref[rows, :], axis=1, keepdims=True),
        )

    def move(j, i):
        src = s2_send.at[j - 1] if i == per else c2_send.at[j - 1, pl.ds(i * lanes, lanes), :]
        dst = s2_recv.at[j - 1] if i == per else c2_recv.at[j - 1, pl.ds(i * lanes, lanes), :]
        spot = (j - 1) * (per + 1) + i
        return pltpu.make_async_remote_copy(
            src_ref=src, dst_ref=dst, send_sem=x2_s.at[spot], recv_sem=x2_r.at[spot],
            device_id={"mp": lax.rem(x + j, mp)}, device_id_type=MESH,
        )

    for j in range(1, mp):
        target = lax.rem(x + j, mp)
        for i in range(per):
            rows = pl.ds(target * part + i * lanes, lanes)
            c2_send[j - 1, i * lanes : (i + 1) * lanes, :] = acc[rows, :].astype(BF16)
            move(j, i).start()
            if i == 0:
                for b in range(per):
                    cut = pl.ds(target * part + b * lanes, lanes)
                    total, pointer = sums(cut)
                    s2_send[j - 1, 0, b : b + 1, :] = to_row(m_ref[cut, :])
                    s2_send[j - 1, 1, b : b + 1, :] = to_row(total)
                    s2_send[j - 1, 2, b : b + 1, :] = to_row(pointer)
                move(j, per).start()

    chunk = min(512, vcols)

    def vocabulary(g, i):
        h = hid[pl.ds(g * part + i * lanes, lanes), :]
        target = tcol[pl.ds(g * half + x * part + i * lanes, lanes), :]
        top = jnp.full((lanes, 128), FLOOR, F32)
        total = jnp.zeros((lanes, 128), F32)
        chosen = jnp.zeros((lanes, 128), F32)
        for q in range(mp):
            for v in range(vcols // chunk):
                w = ow_all[q, :, v * chunk : (v + 1) * chunk]
                logits = jnp.dot(h, w, preferred_element_type=F32)
                first_col = (q * sub + c) * vcols + v * chunk
                ids = (lax.broadcasted_iota(jnp.int32, (1, chunk), 1) + first_col).astype(F32)
                chosen = chosen + lane_sum(jnp.where(ids == target, logits, 0.0))
                new = top
                for b in range(chunk // 128):
                    new = jnp.maximum(new, logits[:, b * 128 : (b + 1) * 128])
                total = total * jnp.exp(top - new)
                for b in range(chunk // 128):
                    total = total + jnp.exp(logits[:, b * 128 : (b + 1) * 128] - new)
                top = new
        row_top = jnp.max(top, axis=1, keepdims=True)
        row_sum = jnp.sum(total * jnp.exp(top - row_top), axis=1, keepdims=True)
        row_hit = jnp.sum(chosen, axis=1, keepdims=True)
        st3[me, g * 3, i : i + 1, :] = to_row(row_top)
        st3[me, g * 3 + 1, i : i + 1, :] = to_row(row_sum)
        st3[me, g * 3 + 2, i : i + 1, :] = to_row(row_hit)

    def hid_copy(i, core):
        block = hid.at[pl.ds(core * part + i * lanes, lanes), :]
        return to_other(block, block, h_s.at[i], h_r.at[i])

    own_sums = [sums(pl.ds(x * part + i * lanes, lanes)) for i in range(per)]
    for j in range(1, mp):
        ow_copy(j, lax.rem(x + mp - j, mp)).wait_recv()
    for j in range(1, mp):
        move(j, per).wait_recv()
    for i in range(per):
        rows = pl.ds(x * part + i * lanes, lanes)
        total, pointer = own_sums[i]
        top = m_ref[rows, :]
        context = acc[rows, :]
        for j in range(1, mp):
            theirs, their_total, their_pointer = [to_col(s2_recv[j - 1, k, i : i + 1, :]) for k in range(3)]
            new = jnp.maximum(top, theirs)
            a, b = jnp.exp(top - new), jnp.exp(theirs - new)
            top = new
            total = total * a + their_total * b
            pointer = pointer * a + their_pointer * b
            move(j, i).wait_recv()
            context = context * a + c2_recv[j - 1, i * lanes : (i + 1) * lanes, :].astype(F32) * b
        hidden = jnp.tanh(frames[rows, :].astype(F32) + context / total).astype(BF16)
        hid[pl.ds(c * part + i * lanes, lanes), :] = hidden
        hid_copy(i, c).start()
        gate = jnp.sum(hidden.astype(F32) * gw_ref[...], axis=1, keepdims=True)
        st3[me, 3 * sub, i : i + 1, :] = to_row(gate)
        st3[me, 3 * sub + 1, i : i + 1, :] = to_row(pointer / total)
        vocabulary(c, i)
        hid_copy(i, other).wait_recv()
        vocabulary(other, i)

    def share(j, slot):
        return pltpu.make_async_remote_copy(
            src_ref=st3.at[slot], dst_ref=st3.at[slot], send_sem=t_s.at[j - 1], recv_sem=t_r.at[j - 1],
            device_id=peer(j), device_id_type=MESH,
        )

    for j in range(1, plane):
        share(j, me).start()
    for j in range(1, plane):
        share(j, lax.rem(me + plane - j, plane)).wait_recv()

    for q in range(mp):
        for g in range(sub):
            one, two = q * sub, q * sub + 1
            top_a, top_b = st3[one, g * 3], st3[two, g * 3]
            top = jnp.maximum(top_a, top_b)
            total = st3[one, g * 3 + 1] * jnp.exp(top_a - top) + st3[two, g * 3 + 1] * jnp.exp(top_b - top)
            log_norm = top + jnp.log(total)
            hit = st3[one, g * 3 + 2] + st3[two, g * 3 + 2]
            gate = 1.0 / (1.0 + jnp.exp(-st3[q * sub + g, 3 * sub]))
            mixed = (1.0 - gate) * jnp.exp(hit - log_norm) + gate * st3[q * sub + g, 3 * sub + 1]
            first_row = (g * mp + q) * per
            out_ref[first_row : first_row + per, :] = -jnp.log(mixed)

    def send_waits(s, carry):
        t = s // PIECES

        @pl.when((z >= t) & (z + 1 < packs))
        def _():
            right(s, z - t).wait_send()

        @pl.when((z + t < packs) & (z > 0))
        def _():
            left(s, z + t).wait_send()

        return carry

    lax.fori_loop(0, (packs - 1) * PIECES, send_waits, 0)

    def core_waits(s, carry):
        across(s // PIECES, lax.rem(s, PIECES), c).wait_send()
        return carry

    lax.fori_loop(0, packs * PIECES, core_waits, 0)
    for i in range(per):
        hid_copy(i, c).wait_send()
    for j in range(1, mp):
        ow_copy(j, x).wait_send()
        for i in range(per + 1):
            move(j, i).wait_send()
    for j in range(1, plane):
        share(j, me).wait_send()


def per_device(
    frame_enc, phrase_enc, key_weight, out_weight, gate_weight,
    phrase_token, bias_blocks, utt_lengths, targets,
):
    packs = lax.axis_size("pack")
    mp = lax.axis_size("mp")
    sub = lax.axis_size("sub")
    plane = mp * sub
    fr, width = frame_enc.shape
    depth = phrase_enc.shape[1]
    own_half = phrase_enc.shape[0] // sub
    vcols = out_weight.shape[1]
    half = fr // sub
    part = half // mp
    lanes = min(part, 128)
    entries = bias_blocks.shape[1]
    hops = (packs - 1) * PIECES
    others = max(mp - 1, 1)
    vmem = pltpu.VMEM
    dma = pltpu.SemaphoreType.DMA
    any_spec = pl.BlockSpec(memory_space=pl.ANY)
    vmem_spec = pl.BlockSpec(memory_space=vmem)
    smem_spec = pl.BlockSpec(memory_space=pltpu.SMEM)
    out = pl.pallas_call(
        functools.partial(kernel, (packs, mp, sub, lanes)),
        out_shape=jax.ShapeDtypeStruct((fr // lanes, lanes), F32),
        in_specs=[any_spec] * 4 + [vmem_spec] * 3 + [smem_spec, vmem_spec],
        out_specs=vmem_spec,
        scratch_shapes=[
            vmem((half, width), BF16),
            vmem((own_half, depth), BF16),
            vmem((depth, width), BF16),
            vmem((packs, PIECES, sub, own_half // PIECES, width), BF16),
            vmem((mp, width, vcols), BF16),
            vmem((fr, 1), F32),
            vmem((entries, 1), F32),
            vmem((packs * PIECES, 8, sub * own_half // PIECES), F32),
            vmem((packs * PIECES, 1, sub * own_half // PIECES), F32),
            vmem((half, 1), F32),
            vmem((half, 128), F32),
            vmem((half, 128), F32),
            vmem((half, width), F32),
            vmem((others, part, width), BF16),
            vmem((others, part, width), BF16),
            vmem((others, 3, part // lanes, lanes), F32),
            vmem((others, 3, part // lanes, lanes), F32),
            vmem((sub * part, width), BF16),
            vmem((plane, 3 * sub + 2, part // lanes, lanes), F32),
            dma((3 + PIECES,)), dma((hops,)), dma((hops,)), dma((hops,)), dma((hops,)),
            dma((packs * PIECES,)), dma((packs * PIECES,)),
            dma((others,)), dma((others,)),
            dma((others * (part // lanes + 1),)), dma((others * (part // lanes + 1),)),
            dma((part // lanes,)), dma((part // lanes,)),
            dma((plane - 1,)), dma((plane - 1,)),
        ],
        compiler_params=pltpu.CompilerParams(
            collective_id=0, has_side_effects=True, vmem_limit_bytes=56 * 1024 * 1024
        ),
    )(
        frame_enc, phrase_enc, key_weight, out_weight,
        gate_weight.reshape(1, width),
        phrase_token.reshape(-1, 128),
        bias_blocks, utt_lengths,
        targets.reshape(-1, 128),
    )
    return out.reshape(fr)


def solution(mesh):
    in_specs = (
        P(("groups", "pack"), None),
        P(("groups", "pack", "mp"), None),
        P(),
        P(None, ("mp", "sub")),
        P(),
        P("groups"),
        P("groups", None),
        P(("groups", "pack"), None),
        P(("groups", "pack")),
    )
    return jax.shard_map(
        per_device, mesh=mesh, in_specs=in_specs, out_specs=P(("groups", "pack")), check_vma=False
    )
```
